512 devices in a mesh: replica: 32 (over z, x_lo), fsdp: 16 (over y, x_hi, core).
Axes of the slice: x: 4 (x_hi: 2, x_lo: 2; x = x_hi * 2 + x_lo), y: 4, z: 16, core: 2. Of those that a mesh axis runs over, the one named last changes fastest.
Arguments:
- hidden: bfloat16 [32, 2048, 8192], P('replica', 'fsdp'), may hold values from -6 to 6
- norm_gain: float32 [8192], replicated, may hold values from 0.1 to 1.9
- dkeys: bfloat16 [32, 2048, 1024], P('replica', 'fsdp'), may hold values from -6 to 6
- local_weights: bfloat16 [32, 8192, 1024], P('replica', 'fsdp'), may hold values from -6 to 6
- outer_params: float32 [8192, 1024], P('fsdp', 'replica'), may hold values from -6 to 6
- momentum: float32 [8192, 1024], P('fsdp', 'replica'), may hold values from -3 to 3
- sync_step: int32 [1], replicated, may hold values from 0 to 15
Outputs:
- next_weights: bfloat16 [32, 8192, 1024], P('replica', 'fsdp')
- outer_next: float32 [8192, 1024], P('fsdp', 'replica')
- momentum_next: float32 [8192, 1024], P('fsdp', 'replica')
The draws below stay inside these ranges and needn't reach their ends.
All inputs are finite; a program needn't handle non-finite values.
Results may differ from the reference program's by a relative error of at most 0.015.
Values may be sent and summed in bfloat16 or wider, within the bound.
A program may use at most 64 MiB of HBM per device.

```python
import jax
import jax.numpy as jnp
from jax import lax

D = 8192
X = 1024
TOKENS = 2048
REPLICAS = 32
WARMUP = 8


def shard_levels(rng, shape, cuts, least, largest):
    def one(axis_at, shards_of):
        heights = jax.random.uniform(jax.random.fold_in(jax.random.fold_in(rng, 6), axis_at), (shards_of,), jnp.float32, least / len(cuts), largest / len(cuts))
        return jnp.repeat(jnp.exp(heights), shape[axis_at] // shards_of).reshape((-1,) + (1,) * (len(shape) - axis_at - 1))

    factor_of = one(*cuts[0])
    for cut in cuts[1:]:
        factor_of = factor_of * one(*cut)
    return factor_of


def gaussian(stream_key, extent, scale, reach, pieces=(), held_as=jnp.bfloat16):
    array = jax.random.normal(stream_key, extent, jnp.float32) * scale
    if len(pieces) > 0:
        array = shard_levels(stream_key, extent, pieces, -0.22, 0.18) * array
    return jnp.clip(array, min=-reach, max=reach).astype(held_as)


def setup_inputs(seed: int = 0) -> dict:
    key_list = jax.random.split(jax.random.key(seed), 8)
    hidden = gaussian(key_list[0], (REPLICAS, TOKENS, D), 1.0, 6.0, ((0, 32), (1, 16)))
    norm_gain = jnp.clip(1.0 + 0.18 * jax.random.normal(key_list[1], (D,), jnp.float32), 0.1, 1.9)
    dkeys = gaussian(key_list[2], (REPLICAS, TOKENS, X), 1.0, 6.0, ((0, 32), (1, 16)))
    local_weights = gaussian(key_list[3], (REPLICAS, D, X), 1.0, 6.0, ((0, 32), (1, 16)))
    outer_params = gaussian(key_list[4], (D, X), 1.0, 6.0, ((0, 16), (1, 32)), jnp.float32)
    momentum = gaussian(key_list[5], (D, X), 0.5, 3.0, ((0, 16), (1, 32)), jnp.float32)
    sync_step = jax.random.randint(key_list[6], (1,), 0, 2 * WARMUP).astype(jnp.int32)
    return {"hidden": hidden, "norm_gain": norm_gain, "dkeys": dkeys, "local_weights": local_weights, "outer_params": outer_params, "momentum": momentum, "sync_step": sync_step}


def reference(hidden, norm_gain, dkeys, local_weights, outer_params, momentum, sync_step):
    scale = 1.0 / D ** 0.5
    total = lax.optimization_barrier(jnp.sum(local_weights.astype(jnp.float32), axis=0))
    average = outer_params - total / REPLICAS
    rate = 0.7 * jnp.minimum(1.0, (sync_step[0].astype(jnp.float32) + 1.0) / WARMUP)
    momentum_next = 0.9 * momentum + average
    outer_next = outer_params - rate * (average + 0.9 * momentum_next)

    def one(items):
        rows, cotangent, weights = items
        values = rows.astype(jnp.float32)
        inverse = lax.rsqrt(lax.optimization_barrier(jnp.mean(values * values, axis=-1, keepdims=True)) + 1e-05)
        normed = (values * inverse * norm_gain).astype(jnp.bfloat16)
        grad = jnp.dot(normed.T, cotangent, preferred_element_type=jnp.float32) * scale
        stepped = weights.astype(jnp.float32) - 1.0 * grad
        return (0.5 * stepped + 0.5 * outer_next).astype(jnp.bfloat16)
    next_weights = lax.map(one, (hidden, dkeys, local_weights))
    return (next_weights, outer_next, momentum_next)
```

```python
import jax
import jax.numpy as jnp
from jax import lax
from jax.experimental import pallas as pl
from jax.experimental.pallas import tpu as pltpu
from jax.sharding import PartitionSpec as P

D = 8192
X = 1024
WARMUP = 8
WORKERS = 32
RING = 16
ROWS = 512
TOK = 128
COLS = X // RING
HALF = COLS // 2
MESH = pl.DeviceIdType.MESH
F32 = jnp.float32
BF16 = jnp.bfloat16

PEERS = [(dy, dx, dc) for dx in (1, 0) for dy in (2, 1, 3, 0) for dc in (0, 1) if (dy, dx, dc) != (0, 0, 0)]


def kernel(
    step, hid, gain, dk, w, outer, mom,
    merged, outer_new, mom_new,
    hid_v, gain_v, dk_v, w_v, outer_v, mom_v,
    inv_v, send_v, norm_v, keys_v, wt, down, up, tot, xs, xr, gathered, acc, out_v, on_v, mn_v,
    load_sem, store_sem, a2a_s, a2a_r, key_s, key_r, rs_s, rs_r, x_s, x_r, ag_s, ag_r,
):
    rep, fs = lax.axis_index("replica"), lax.axis_index("fsdp")
    z, xl = rep // 2, rep % 2
    y, xh, core = fs // 4, (fs // 2) % 2, fs % 2

    def fs_at(dy, dx, dc):
        return ((y + dy) % 4) * 4 + ((xh + dx) % 2) * 2 + (core + dc) % 2

    def ring(dz):
        return (z + dz + RING) % RING

    def in_group(dy, dx, dc):
        return (rep, fs_at(dy, dx, dc))

    z_next, z_prev = (ring(1) * 2 + xl, fs), (ring(-1) * 2 + xl, fs)
    partner = (z * 2 + 1 - xl, fs)

    barrier = pltpu.get_barrier_semaphore()
    others = [in_group(*d) for d in PEERS] + [z_next, z_prev, partner]
    for dev in others:
        pl.semaphore_signal(barrier, inc=1, device_id=dev, device_id_type=MESH)

    loads = [
        pltpu.make_async_copy(a, b, load_sem.at[i])
        for i, (a, b) in enumerate(
            [(w, w_v), (dk, dk_v), (hid, hid_v), (gain, gain_v), (outer, outer_v), (mom, mom_v)]
        )
    ]
    for cp in loads:
        cp.start()

    started = []

    def send(src, dst, ss, rs, dev):
        cp = pltpu.make_async_remote_copy(
            src_ref=src, dst_ref=dst, send_sem=ss, recv_sem=rs, device_id=dev, device_id_type=MESH
        )
        cp.start()
        started.append(cp)
        return cp

    loads[0].wait()

    @pl.loop(0, X // 128)
    def _(j):
        cols = pl.ds(pl.multiple_of(j * 128, 128), 128)
        wt[cols, :] = w_v[:, cols].T

    loads[1].wait()
    for j in range(X // 128):
        keys_v[fs, pl.ds(j * 128, 128), :] = dk_v[:, j * 128 : (j + 1) * 128].T

    pl.semaphore_wait(barrier, len(others))

    def chunk(dz):
        return pl.ds(pl.multiple_of(ring(dz) * COLS, COLS), COLS)

    def rs_down(s):
        if s == 0:
            src = wt.at[chunk(-8)]
        else:
            rs_copies[("d", s - 1)].wait_recv()
            down[s - 1] = (down[s - 1].astype(F32) + wt[chunk(s - 8), :].astype(F32)).astype(BF16)
            src = down.at[s - 1]
        rs_copies[("d", s)] = send(src, down.at[s], rs_s.at[s], rs_r.at[s], z_prev)

    def rs_up(s):
        if s == 0:
            src = wt.at[chunk(7)]
        else:
            rs_copies[("u", s - 1)].wait_recv()
            up[s - 1] = (up[s - 1].astype(F32) + wt[chunk(7 - s), :].astype(F32)).astype(BF16)
            src = up.at[s - 1]
        rs_copies[("u", s)] = send(src, up.at[s], rs_s.at[8 + s], rs_r.at[8 + s], z_next)

    rs_copies = {}

    def rs_step(s):
        rs_down(s)
        if s < 7:
            rs_up(s)

    n_key = [0]
    key_copies = {}

    def key_send(name, src_slot, rows, to):
        i = n_key[0]
        n_key[0] += 1
        part = keys_v.at[src_slot, rows]
        key_copies[name] = send(part, part, key_s.at[i], key_r.at[i], in_group(*to))

    whole, first, second = pl.ds(0, X), pl.ds(0, X // 2), pl.ds(X // 2, X // 2)

    def keys_own():
        key_send("x", fs, whole, (0, 1, 0))
        key_send("up0", fs, whole, (1, 0, 0))
        key_send("down0", fs, whole, (3, 0, 0))
        key_send("c00", fs, whole, (0, 0, 1))

    def keys_x():
        key_copies["x"].wait_recv()
        slot = fs_at(0, 1, 0)
        key_send("up1", slot, whole, (1, 0, 0))
        key_send("down1", slot, whole, (3, 0, 0))
        key_send("c01", slot, whole, (0, 0, 1))

    def keys_y(dx):
        key_copies["up%d" % dx].wait_recv()
        slot = fs_at(3, dx, 0)
        key_send("upup%d" % dx, slot, first, (1, 0, 0))
        key_send("c3%d" % dx, slot, whole, (0, 0, 1))
        key_copies["down%d" % dx].wait_recv()
        slot = fs_at(1, dx, 0)
        key_send("downdown%d" % dx, slot, second, (3, 0, 0))
        key_send("c1%d" % dx, slot, whole, (0, 0, 1))

    def keys_far(dx):
        key_copies["upup%d" % dx].wait_recv()
        key_copies["downdown%d" % dx].wait_recv()
        key_send("c2%d" % dx, fs_at(2, dx, 0), whole, (0, 0, 1))

    def keys_core():
        for dy in range(4):
            for dx in range(2):
                key_copies["c%d%d" % (dy, dx)].wait_recv()

    def statistics():
        loads[2].wait()
        loads[3].wait()

        @pl.loop(0, TOK // 16)
        def _(i):
            rows = pl.ds(pl.multiple_of(i * 16, 16), 16)
            total = jnp.zeros((16, 512), F32)
            for b in range(D // 512):
                v = hid_v[rows, b * 512 : (b + 1) * 512].astype(F32)
                total = total + v * v
            mean = jnp.sum(total, axis=-1, keepdims=True) * (1.0 / D)
            inv_v[rows, :] = jnp.broadcast_to(lax.rsqrt(mean + 1e-05), (16, 128))

    def normed(b, k):
        cols = pl.ds(pl.multiple_of(b * ROWS + k * 128, 128), 128)
        return (hid_v[:, cols].astype(F32) * inv_v[...] * gain_v[:, cols]).astype(BF16)

    a2a = []

    def a2a_send(i):
        b = fs_at(*PEERS[i])
        for k in range(ROWS // 128):
            send_v[b, :, k * 128 : (k + 1) * 128] = normed(b, k)
        a2a.append(send(send_v.at[b], norm_v.at[fs], a2a_s.at[i], a2a_r.at[i], in_group(*PEERS[i])))

    def own_block():
        for k in range(ROWS // 128):
            norm_v[fs, :, k * 128 : (k + 1) * 128] = normed(fs, k)

    def multiply(base, n, add):
        @pl.loop(0, 4)
        def _(i):
            rows = pl.ds(pl.multiple_of(i * (X // 4), X // 4), X // 4)
            left = jnp.concatenate([keys_v[base + q, rows, :] for q in range(n)], axis=1)
            right = norm_v[base : base + n].reshape(n * TOK, ROWS)
            part = jnp.dot(left, right, preferred_element_type=F32)
            acc[rows, :] = acc[rows, :] + part if add else part

    def update():
        rs_copies[("d", 7)].wait_recv()
        rs_copies[("u", 6)].wait_recv()
        tot[...] = wt[chunk(0), :].astype(F32) + down[7].astype(F32) + up[6].astype(F32)
        mine = pl.ds(pl.multiple_of(xl * HALF, HALF), HALF)
        theirs = pl.ds(pl.multiple_of((1 - xl) * HALF, HALF), HALF)
        xs[...] = tot[theirs, :]
        cp = send(xs, xr, x_s.at[0], x_r.at[0], partner)
        loads[4].wait()
        loads[5].wait()
        rate = 0.7 * jnp.minimum(1.0, (step[0].astype(F32) + 1.0) / WARMUP)
        cp.wait_recv()
        average = outer_v[...] - (tot[mine, :] + xr[...]) / WORKERS
        momentum = 0.9 * mom_v[...] + average
        new = outer_v[...] - rate * (average + 0.9 * momentum)
        mn_v[...] = momentum
        on_v[...] = new
        gathered[pl.ds(pl.multiple_of(z * COLS + xl * HALF, HALF), HALF), :] = new.astype(BF16)

    def piece(dz, other):
        half = 1 - xl if other else xl
        return pl.ds(pl.multiple_of(ring(dz) * COLS + half * HALF, HALF), HALF)

    ag = {}

    def ag_send(way, s, other):
        i = (way * 8 + s) * 2 + other
        part = gathered.at[piece(-s if way == 0 else s, other)]
        ag[(way, s, other)] = send(part, part, ag_s.at[i], ag_r.at[i], z_next if way == 0 else z_prev)

    def ag_step(s):
        for other in (0, 1):
            for way in (0, 1):
                if s > 0 and not (way == 1 and s > 7):
                    ag[(way, s - 1, other)].wait_recv()
                if s < (8, 7)[way]:
                    if s == 0 and other == 1 and way == 0:
                        x_ag.wait_recv()
                    ag_send(way, s, other)

    def finish(dm, n):
        m = (z // 2 + dm + 8) % 8
        rows = pl.ds(pl.multiple_of(m * 128, 128), 128)
        scale = 1.0 / D**0.5
        stepped = wt[rows, :].astype(F32) - 1.0 * (acc[rows, :] * scale)
        out_v[:, rows] = (0.5 * stepped + 0.5 * gathered[rows, :].astype(F32)).astype(BF16).T
        cp = pltpu.make_async_copy(out_v.at[:, rows], merged.at[:, rows], store_sem.at[n])
        cp.start()
        stores.append(cp)

    stores = []

    rs_step(0)
    keys_own()
    statistics()
    for i in range(0, 6):
        a2a_send(i)
    rs_step(1)
    for i in range(6, 15):
        a2a_send(i)
    own_block()
    rs_step(2)
    keys_x()
    rs_step(3)
    keys_y(0)
    rs_step(4)
    rs_step(5)
    keys_y(1)
    rs_step(6)
    rs_step(7)
    keys_far(0)
    update()
    x_ag = send(gathered.at[piece(0, 0)], gathered.at[piece(0, 0)], x_s.at[1], x_r.at[1], partner)
    ag_step(0)
    for i, (a, b) in enumerate([(on_v, outer_new), (mn_v, mom_new)]):
        cp = pltpu.make_async_copy(a, b, store_sem.at[8 + i])
        cp.start()
        stores.append(cp)
    keys_far(1)
    ag_step(1)
    ag_step(2)
    ag_step(3)
    keys_core()
    for cp in a2a:
        cp.wait_recv()
    ag_step(4)
    multiply(0, 8, False)
    ag_step(5)
    multiply(8, 8, True)
    ag_step(6)
    for n, dm in enumerate([0, 1, -1]):
        finish(dm, n)
    ag_step(7)
    for n, dm in enumerate([2, -2, 3, -3]):
        finish(dm, 3 + n)
    ag_step(8)
    finish(4, 7)
    for cp in stores:
        cp.wait()
    for cp in started:
        cp.wait_send()


def on_device(hidden, norm_gain, dkeys, local_weights, outer_params, momentum, sync_step):
    any_ = pl.BlockSpec(memory_space=pltpu.HBM)
    dma = pltpu.SemaphoreType.DMA
    merged, outer_new, mom_new = pl.pallas_call(
        kernel,
        out_shape=[
            jax.ShapeDtypeStruct((ROWS, X), BF16),
            jax.ShapeDtypeStruct((HALF, ROWS), F32),
            jax.ShapeDtypeStruct((HALF, ROWS), F32),
        ],
        in_specs=[pl.BlockSpec(memory_space=pltpu.SMEM)] + [any_] * 6,
        out_specs=[any_] * 3,
        scratch_shapes=[
            pltpu.VMEM((TOK, D), BF16),
            pltpu.VMEM((1, D), F32),
            pltpu.VMEM((TOK, X), BF16),
            pltpu.VMEM((ROWS, X), BF16),
            pltpu.VMEM((HALF, ROWS), F32),
            pltpu.VMEM((HALF, ROWS), F32),
            pltpu.VMEM((TOK, 128), F32),
            pltpu.VMEM((16, TOK, ROWS), BF16),
            pltpu.VMEM((16, TOK, ROWS), BF16),
            pltpu.VMEM((16, X, TOK), BF16),
            pltpu.VMEM((X, ROWS), BF16),
            pltpu.VMEM((8, COLS, ROWS), BF16),
            pltpu.VMEM((7, COLS, ROWS), BF16),
            pltpu.VMEM((COLS, ROWS), F32),
            pltpu.VMEM((HALF, ROWS), F32),
            pltpu.VMEM((HALF, ROWS), F32),
            pltpu.VMEM((X, ROWS), BF16),
            pltpu.VMEM((X, ROWS), F32),
            pltpu.VMEM((ROWS, X), BF16),
            pltpu.VMEM((HALF, ROWS), F32),
            pltpu.VMEM((HALF, ROWS), F32),
            dma((6,)), dma((10,)), dma((15,)), dma((15,)), dma((17,)), dma((17,)),
            dma((15,)), dma((15,)), dma((2,)), dma((2,)), dma((32,)), dma((32,)),
        ],
        compiler_params=pltpu.CompilerParams(
            collective_id=0, has_side_effects=True, vmem_limit_bytes=60 << 20
        ),
        name="outer_sync",
    )(
        sync_step, hidden[0], norm_gain.reshape(1, D), dkeys[0], local_weights[0],
        outer_params.T, momentum.T,
    )
    return merged[None], outer_new.T, mom_new.T


def solution(mesh):
    placed = (
        P("replica", "fsdp", None),
        P(),
        P("replica", "fsdp", None),
        P("replica", "fsdp", None),
        P("fsdp", "replica"),
        P("fsdp", "replica"),
        P(),
    )
    return jax.shard_map(
        on_device,
        mesh=mesh,
        in_specs=placed,
        out_specs=(P("replica", "fsdp", None), P("fsdp", "replica"), P("fsdp", "replica")),
        check_vma=False,
    )
```

```python
import jax
import jax.numpy as jnp
from jax import lax
from jax.experimental import pallas as pl
from jax.experimental.pallas import tpu as pltpu
from jax.sharding import PartitionSpec as P

D = 8192
X = 1024
WARMUP = 8
WORKERS = 32
RING = 16
ROWS = 512
TOK = 128
COLS = X // RING
HALF = COLS // 2
MESH = pl.DeviceIdType.MESH
F32 = jnp.float32
BF16 = jnp.bfloat16

SAME = [(dy, dx, 0) for dx in (1, 0) for dy in (2, 1, 3, 0) if (dy, dx) != (0, 0)]
CROSS = [(dy, dx, 1) for dx in (1, 0) for dy in (2, 1, 3, 0)]
PLACES = [p for pair in zip(SAME, CROSS) for p in pair] + CROSS[7:]
CHAINS = [(-1, (8, 6, 4, 2)), (-1, (7, 5, 3, 1)), (1, (7, 5, 3, 1)), (1, (6, 4, 2))]
AG_FAR = {1: 8, -1: 7}
PAIR_ORDER = [way * c[k] for k in range(4) for way, c in CHAINS if k < len(c)] + [0]


def kernel(
    step, hid, gain, dk, w, outer, mom,
    merged, outer_new, mom_new,
    hid_v, gain_v, dk_v, w_v, outer_v, mom_v,
    inv_v, send_v, norm_v, keys_v, wt, pair_v, first_v, chain_v, gathered, acc, out_v, on_v, mn_v,
    load_sem, store_sem, a2a_s, a2a_r, key_s, key_r, pair_s, pair_r, rs_s, rs_r, x_s, x_r, ag_s, ag_r,
):
    rep, fs = lax.axis_index("replica"), lax.axis_index("fsdp")
    z, xl = rep // 2, rep % 2
    y, xh, core = fs // 4, (fs // 2) % 2, fs % 2

    def ring(dz):
        return (z + dz + RING) % RING

    def in_group(dy, dx, dc):
        return (rep, ((y + dy) % 4) * 4 + ((xh + dx) % 2) * 2 + (core + dc) % 2)

    def on_ring(dz):
        return (ring(dz) * 2 + xl, fs)

    def slot(dy, dx, dc):
        return ((core + dc) % 2) * 8 + ((y + dy) % 4) * 2 + (xh + dx) % 2

    partner = (z * 2 + 1 - xl, fs)

    barrier = pltpu.get_barrier_semaphore()
    others = [in_group(*d) for d in SAME + CROSS] + [on_ring(d) for d in (1, -1, 2, -2)] + [partner]
    for dev in others:
        pl.semaphore_signal(barrier, inc=1, device_id=dev, device_id_type=MESH)

    loads = [
        pltpu.make_async_copy(a, b, load_sem.at[i])
        for i, (a, b) in enumerate(
            [(w, w_v), (dk, dk_v), (hid, hid_v), (gain, gain_v), (outer, outer_v), (mom, mom_v)]
        )
    ]
    for cp in loads:
        cp.start()

    started = []

    def send(src, dst, ss, rs, dev):
        cp = pltpu.make_async_remote_copy(
            src_ref=src, dst_ref=dst, send_sem=ss, recv_sem=rs, device_id=dev, device_id_type=MESH
        )
        cp.start()
        started.append(cp)
        return cp

    def turn_weights():
        loads[0].wait()

        @pl.loop(0, X // 128)
        def _(j):
            cols = pl.ds(pl.multiple_of(j * 128, 128), 128)
            wt[cols, :] = w_v[:, cols].T

    def turn_keys():
        loads[1].wait()
        for j in range(X // 128):
            keys_v[slot(0, 0, 0), pl.ds(j * 128, 128), :] = dk_v[:, j * 128 : (j + 1) * 128].T

    def owned(dz, half):
        return pl.ds(pl.multiple_of(ring(dz) * COLS + half * HALF, HALF), HALF)

    pairs = {}

    def pair_send(dz):
        i = len(pairs)
        pairs[dz] = send(wt.at[owned(dz, 1 - xl)], pair_v.at[ring(dz)], pair_s.at[i], pair_r.at[i], partner)

    def pair_sum(dz):
        pairs[dz].wait_recv()
        return wt[owned(dz, xl), :].astype(F32) + pair_v[ring(dz)].astype(F32)

    links = {}

    def rs_step(k):
        for n, (way, distances) in enumerate(CHAINS):
            if k >= len(distances):
                continue
            d = distances[k]
            i = n * 4 + k
            part = pair_sum(way * d)
            if k == 0:
                src, at = first_v.at[n], (first_v, n)
            else:
                links[(n, k - 1)].wait_recv()
                src, at = chain_v.at[i - 1], (chain_v, i - 1)
                part = part + chain_v[i - 1].astype(F32)
            at[0][at[1]] = part.astype(BF16)
            links[(n, k)] = send(src, chain_v.at[i], rs_s.at[i], rs_r.at[i], on_ring(way * min(d, 2)))

    def update():
        total = pair_sum(0)
        for n, (_, distances) in enumerate(CHAINS):
            k = len(distances) - 1
            links[(n, k)].wait_recv()
            total = total + chain_v[n * 4 + k].astype(F32)
        loads[4].wait()
        loads[5].wait()
        rate = 0.7 * jnp.minimum(1.0, (step[0].astype(F32) + 1.0) / WARMUP)
        average = outer_v[...] - total / WORKERS
        momentum = 0.9 * mom_v[...] + average
        new = outer_v[...] - rate * (average + 0.9 * momentum)
        mn_v[...] = momentum
        on_v[...] = new
        gathered[owned(0, xl), :] = new.astype(BF16)

    ag, crossed = {}, {}

    def ag_send(way, d):
        hop = 1 if d == -1 else 2
        far = max(d, 0) + hop
        i = (far - 1) * 2 + (way + 1) // 2
        part = gathered.at[owned(-way * max(d, 0), xl)]
        ag[(way, far)] = send(part, part, ag_s.at[i], ag_r.at[i], on_ring(way * hop))

    def cross(way, d):
        i = d * 2 + (way + 1) // 2
        part = gathered.at[owned(-way * d, xl)]
        crossed[(way, d)] = send(part, part, x_s.at[i], x_r.at[i], partner)

    def ag_start():
        for d in (-1, 0):
            for way in (1, -1):
                ag_send(way, d)
        cross(1, 0)

    def ag_step(k):
        for d in (2 * k + 1, 2 * k + 2):
            for way in (1, -1):
                if d <= AG_FAR[way]:
                    ag[(way, d)].wait_recv()
                    if d + 2 <= AG_FAR[way]:
                        ag_send(way, d)
                    cross(way, d)

    def ag_crossed():
        for cp in crossed.values():
            cp.wait_recv()

    key_copies = {}

    def key_send(name, place, rows, to):
        i = len(key_copies)
        part = keys_v.at[slot(*place), rows]
        key_copies[name] = send(part, part, key_s.at[i], key_r.at[i], in_group(*to))

    whole, first, second = pl.ds(0, X), pl.ds(0, X // 2), pl.ds(X // 2, X // 2)

    def keys_own():
        key_send("x", (0, 0, 0), whole, (0, 1, 0))
        key_send("up0", (0, 0, 0), whole, (1, 0, 0))
        key_send("down0", (0, 0, 0), whole, (3, 0, 0))

    def keys_x():
        key_copies["x"].wait_recv()
        key_send("up1", (0, 1, 0), whole, (1, 0, 0))
        key_send("down1", (0, 1, 0), whole, (3, 0, 0))
        key_send("c01", (0, 1, 0), whole, (0, 0, 1))

    def keys_y(dx):
        key_copies["up%d" % dx].wait_recv()
        key_send("upup%d" % dx, (3, dx, 0), first, (1, 0, 0))
        key_send("c3%d" % dx, (3, dx, 0), whole, (0, 0, 1))
        key_copies["down%d" % dx].wait_recv()
        key_send("downdown%d" % dx, (1, dx, 0), second, (3, 0, 0))
        key_send("c1%d" % dx, (1, dx, 0), whole, (0, 0, 1))

    def keys_far(dx):
        key_copies["upup%d" % dx].wait_recv()
        key_copies["downdown%d" % dx].wait_recv()
        key_send("c2%d" % dx, (2, dx, 0), whole, (0, 0, 1))

    def statistics():
        loads[2].wait()
        loads[3].wait()

        @pl.loop(0, TOK // 16)
        def _(i):
            rows = pl.ds(pl.multiple_of(i * 16, 16), 16)
            total = jnp.zeros((16, 512), F32)
            for b in range(D // 512):
                v = hid_v[rows, b * 512 : (b + 1) * 512].astype(F32)
                total = total + v * v
            mean = jnp.sum(total, axis=-1, keepdims=True) * (1.0 / D)
            inv_v[rows, :] = jnp.broadcast_to(lax.rsqrt(mean + 1e-05), (16, 128))

    def normed(b, k):
        cols = pl.ds(pl.multiple_of(b * ROWS + k * 128, 128), 128)
        return (hid_v[:, cols].astype(F32) * inv_v[...] * gain_v[:, cols]).astype(BF16)

    a2a = {}

    def a2a_send(place):
        i = len(a2a)
        dev = in_group(*place)
        for k in range(ROWS // 128):
            send_v[i, :, k * 128 : (k + 1) * 128] = normed(dev[1], k)
        a2a[place] = send(send_v.at[i], norm_v.at[slot(0, 0, 0)], a2a_s.at[i], a2a_r.at[i], dev)

    def own_block():
        for k in range(ROWS // 128):
            norm_v[slot(0, 0, 0), :, k * 128 : (k + 1) * 128] = normed(fs, k)

    def multiply(dc):
        base = ((core + dc) % 2) * 8

        @pl.loop(0, 4)
        def _(i):
            rows = pl.ds(pl.multiple_of(i * (X // 4), X // 4), X // 4)
            left = jnp.concatenate([keys_v[base + q, rows, :] for q in range(8)], axis=1)
            right = norm_v[pl.ds(base, 8)].reshape(8 * TOK, ROWS)
            part = jnp.dot(left, right, preferred_element_type=F32)
            acc[rows, :] = acc[rows, :] + part if dc else part

    def grad_same():
        for place in SAME:
            a2a[place].wait_recv()
        multiply(0)

    def grad_cross():
        for place in CROSS:
            a2a[place].wait_recv()
        for dy in range(4):
            for dx in range(2):
                key_copies["c%d%d" % (dy, dx)].wait_recv()
        multiply(1)

    stores = []

    def store(src, dst):
        cp = pltpu.make_async_copy(src, dst, store_sem.at[len(stores)])
        cp.start()
        stores.append(cp)

    def finish(dm):
        m = (z // 2 + dm + 8) % 8
        rows = pl.ds(pl.multiple_of(m * 128, 128), 128)
        scale = 1.0 / D**0.5
        stepped = wt[rows, :].astype(F32) - 1.0 * (acc[rows, :] * scale)
        out_v[:, rows] = (0.5 * stepped + 0.5 * gathered[rows, :].astype(F32)).astype(BF16).T
        store(out_v.at[:, rows], merged.at[:, rows])

    turn_weights()
    pl.semaphore_wait(barrier, len(others))
    for dz in PAIR_ORDER:
        pair_send(dz)
    turn_keys()
    keys_own()
    key_send("c00", (0, 0, 0), whole, (0, 0, 1))
    statistics()
    for place in PLACES[:6]:
        a2a_send(place)
    rs_step(0)
    for place in PLACES[6:11]:
        a2a_send(place)
    rs_step(1)
    for place in PLACES[11:]:
        a2a_send(place)
    own_block()
    rs_step(2)
    keys_x()
    rs_step(3)
    keys_y(0)
    update()
    ag_start()
    store(on_v, outer_new)
    store(mn_v, mom_new)
    keys_y(1)
    ag_step(0)
    keys_far(0)
    ag_step(1)
    keys_far(1)
    ag_step(2)
    ag_step(3)
    grad_same()
    grad_cross()
    ag_crossed()
    for dm in (0, 1, -1, 2, -2, 3, -3, 4):
        finish(dm)
    for cp in stores:
        cp.wait()
    for cp in started:
        cp.wait_send()


def copy_kernel(merged, outer_new, mom_new, merged_out, outer_out, mom_out, merged_v, outer_v, mom_v, in_sem, out_sem):
    routes = [(merged.at[r], merged_v.at[r], merged_out.at[r]) for r in (pl.ds(128 * i, 128) for i in range(4))]
    routes += [(outer_new, outer_v, outer_out), (mom_new, mom_v, mom_out)]
    arrive = [pltpu.make_async_copy(a, b, in_sem.at[i]) for i, (a, b, _) in enumerate(routes)]
    leave = [pltpu.make_async_copy(b, c, out_sem.at[i]) for i, (_, b, c) in enumerate(routes)]
    for cp in arrive:
        cp.start()
    for a, b in zip(arrive, leave):
        a.wait()
        b.start()
    for cp in leave:
        cp.wait()


def on_device(hidden, norm_gain, dkeys, local_weights, outer_params, momentum, sync_step):
    any_ = pl.BlockSpec(memory_space=pltpu.HBM)
    dma = pltpu.SemaphoreType.DMA
    merged, outer_new, mom_new = pl.pallas_call(
        kernel,
        out_shape=[
            jax.ShapeDtypeStruct((ROWS, X), BF16),
            jax.ShapeDtypeStruct((HALF, ROWS), F32),
            jax.ShapeDtypeStruct((HALF, ROWS), F32),
        ],
        in_specs=[pl.BlockSpec(memory_space=pltpu.SMEM)] + [any_] * 6,
        out_specs=[any_] * 3,
        scratch_shapes=[
            pltpu.VMEM((TOK, D), BF16),
            pltpu.VMEM((1, D), F32),
            pltpu.VMEM((TOK, X), BF16),
            pltpu.VMEM((ROWS, X), BF16),
            pltpu.VMEM((HALF, ROWS), F32),
            pltpu.VMEM((HALF, ROWS), F32),
            pltpu.VMEM((TOK, 128), F32),
            pltpu.VMEM((16, TOK, ROWS), BF16),
            pltpu.VMEM((16, TOK, ROWS), BF16),
            pltpu.VMEM((16, X, TOK), BF16),
            pltpu.VMEM((X, ROWS), BF16),
            pltpu.VMEM((RING, HALF, ROWS), BF16),
            pltpu.VMEM((4, HALF, ROWS), BF16),
            pltpu.VMEM((15, HALF, ROWS), BF16),
            pltpu.VMEM((X, ROWS), BF16),
            pltpu.VMEM((X, ROWS), F32),
            pltpu.VMEM((ROWS, X), BF16),
            pltpu.VMEM((HALF, ROWS), F32),
            pltpu.VMEM((HALF, ROWS), F32),
            dma((6,)), dma((10,)), dma((15,)), dma((15,)), dma((17,)), dma((17,)), dma((16,)), dma((16,)),
            dma((15,)), dma((15,)), dma((18,)), dma((18,)), dma((16,)), dma((16,)),
        ],
        compiler_params=pltpu.CompilerParams(
            collective_id=0, has_side_effects=True, vmem_limit_bytes=60 << 20
        ),
        name="outer_sync",
    )(
        sync_step, hidden[0], norm_gain.reshape(1, D), dkeys[0], local_weights[0],
        outer_params.T, momentum.T,
    )
    results = [merged, outer_new, mom_new]
    merged, outer_new, mom_new = pl.pallas_call(
        copy_kernel,
        out_shape=[jax.ShapeDtypeStruct(a.shape, a.dtype) for a in results],
        in_specs=[any_] * 3,
        out_specs=[any_] * 3,
        scratch_shapes=[pltpu.VMEM(a.shape, a.dtype) for a in results] + [dma((6,)), dma((6,))],
        compiler_params=pltpu.CompilerParams(vmem_limit_bytes=60 << 20),
        name="results",
    )(*results)
    return merged[None], outer_new.T, mom_new.T


def solution(mesh):
    placed = (
        P("replica", "fsdp", None),
        P(),
        P("replica", "fsdp", None),
        P("replica", "fsdp", None),
        P("fsdp", "replica"),
        P("fsdp", "replica"),
        P(),
    )
    return jax.shard_map(
        on_device,
        mesh=mesh,
        in_specs=placed,
        out_specs=(P("replica", "fsdp", None), P("fsdp", "replica"), P("fsdp", "replica")),
        check_vma=False,
    )
```

```python
import jax
import jax.numpy as jnp
from jax import lax
from jax.experimental import pallas as pl
from jax.experimental.pallas import tpu as pltpu
from jax.sharding import PartitionSpec as P

D = 8192
X = 1024
WARMUP = 8
WORKERS = 32
RING = 16
ROWS = 512
TOK = 128
COLS = X // RING
HALF = COLS // 2
MESH = pl.DeviceIdType.MESH
F32 = jnp.float32
BF16 = jnp.bfloat16

PLACES = [(dy, dx, dc) for dx in (0, 1) for dy in (2, 1, 3, 0) for dc in (0, 1) if (dy, dx, dc) != (0, 0, 0)]
CHAINS = [(-1, (8, 6, 4, 2)), (-1, (7, 5, 3, 1)), (1, (7, 5, 3, 1)), (1, (6, 4, 2))]
AG_FAR = {1: 8, -1: 7}
PAIR_ORDER = [way * c[k] for k in range(4) for way, c in CHAINS if k < len(c)] + [0]
KEYS = ["own", "x"] + [n + d for d in "01" for n in ("up", "down", "upup", "downdown", "s3", "s1", "s2")] + ["s01"]


def kernel(
    step, hid, gain, dk, w, outer, mom,
    merged, outer_new, mom_new,
    hid_v, gain_v, dk_v, w_v, outer_v, mom_v,
    inv_v, send_v, norm_v, keys_v, wt, other_wt, pair_v, first_v, chain_v, gathered, acc, out_v, on_v, mn_v,
    load_sem, store_sem, a2a_s, a2a_r, key_s, key_r, pair_s, pair_r, core_s, core_r,
    rs_s, rs_r, ag_s, ag_r, x_s, x_r, c_s, c_r, go_sem,
):
    rep, fs = lax.axis_index("replica"), lax.axis_index("fsdp")
    z, xl = rep // 2, rep % 2
    y, xh, core = fs // 4, (fs // 2) % 2, fs % 2

    def ring(dz):
        return (z + dz + RING) % RING

    def in_group(dy, dx, dc):
        return (rep, ((y + dy) % 4) * 4 + ((xh + dx) % 2) * 2 + (core + dc) % 2)

    def on_ring(dz):
        return (ring(dz) * 2 + xl, fs)

    def chip(dy, dx):
        return ((xh + dx) % 2) * 4 + (y + dy) % 4

    sibling = (rep, fs + 1 - 2 * core)
    partner = (z * 2 + 1 - xl, fs)
    across = (z * 2 + 1 - xl, fs + 1 - 2 * core)

    barrier = pltpu.get_barrier_semaphore()
    group = [(rep, (fs // 2 + i) % 8 * 2) for i in range(8)] + [(partner[0], fs - core)]
    along = [on_ring(d) for d in (1, -1, 2, -2)]

    def greet(dev):
        pl.semaphore_signal(barrier, inc=1, device_id=dev, device_id_type=MESH)

    for dev in group[1:]:
        greet(dev)

    @pl.when(core == 1)
    def _():
        greet(group[0])
        for dev in along:
            greet(dev)

    def group_is_in():
        @pl.when(core == 0)
        def _():
            pl.semaphore_wait(barrier, 17)
            pl.semaphore_signal(go_sem, inc=1, device_id=sibling, device_id_type=MESH)

        @pl.when(core == 1)
        def _():
            pl.semaphore_wait(go_sem, 1)

    def neighbours_are_in():
        pl.semaphore_wait(barrier, len(along))

    loads = [
        pltpu.make_async_copy(a, b, load_sem.at[i])
        for i, (a, b) in enumerate(
            [
                (w, w_v), (dk, dk_v), (hid, hid_v), (gain, gain_v),
                (outer, outer_v.at[core]), (mom, mom_v.at[core]),
            ]
        )
    ]
    for cp in loads:
        cp.start()

    loads[0].wait()

    @pl.loop(0, X // 128)
    def _(j):
        cols = pl.ds(pl.multiple_of(j * 128, 128), 128)
        wt[pl.ds(2 * j, 2)] = w_v[:, cols].T.reshape(2, 2, HALF, ROWS)

    loads[1].wait()
    for j in range(X // 128):
        keys_v[chip(0, 0), core, pl.ds(j * 128, 128), :] = dk_v[:, j * 128 : (j + 1) * 128].T

    for cp in loads[2:]:
        cp.wait()

    group_is_in()

    started = []

    def send(src, dst, ss, rs, dev):
        cp = pltpu.make_async_remote_copy(
            src_ref=src, dst_ref=dst, send_sem=ss, recv_sem=rs, device_id=dev, device_id_type=MESH
        )
        cp.start()
        started.append(cp)

    def arrive(dst, rs):
        pltpu.make_async_remote_copy(
            src_ref=dst, dst_ref=dst, send_sem=rs, recv_sem=rs, device_id=sibling, device_id_type=MESH
        ).wait_recv()

    def pair_send(to):
        for i, dz in enumerate(PAIR_ORDER):
            t = ring(dz)
            send(wt.at[t, 1 - xl], pair_v.at[core, t], pair_s.at[i], pair_r.at[core, i], to)

    def pair_sum(dz):
        t, i = ring(dz), PAIR_ORDER.index(dz)
        for c in (0, 1):
            arrive(pair_v.at[c, t], pair_r.at[c, i])
        return [
            other_wt[t].astype(F32) + pair_v[0, t].astype(F32),
            wt[t, xl].astype(F32) + pair_v[1, t].astype(F32),
        ]

    def rs_step(k):
        for n, (way, distances) in enumerate(CHAINS):
            if k >= len(distances):
                continue
            d = distances[k]
            i = n * 4 + k
            parts = pair_sum(way * d)
            if k == 0:
                buffer, at = first_v, n
            else:
                buffer, at = chain_v, i - 1
                arrive(chain_v.at[i - 1], rs_r.at[i - 1])
            for c in (0, 1):
                part = parts[c] if k == 0 else parts[c] + chain_v[i - 1, c].astype(F32)
                buffer[at, c] = part.astype(BF16)
            send(buffer.at[at], chain_v.at[i], rs_s.at[i], rs_r.at[i], on_ring(way * min(d, 2)))

    def update():
        totals = pair_sum(0)
        for n, (_, distances) in enumerate(CHAINS):
            i = n * 4 + len(distances) - 1
            arrive(chain_v.at[i], rs_r.at[i])
            totals = [totals[c] + chain_v[i, c].astype(F32) for c in (0, 1)]
        rate = 0.7 * jnp.minimum(1.0, (step[0].astype(F32) + 1.0) / WARMUP)
        arrive(outer_v.at[0], core_r.at[1])
        arrive(mom_v.at[0], core_r.at[2])
        for c in (0, 1):
            average = outer_v[c] - totals[c] / WORKERS
            momentum = 0.9 * mom_v[c] + average
            new = outer_v[c] - rate * (average + 0.9 * momentum)
            mn_v[c] = momentum
            on_v[c] = new
            gathered[z, xl, c] = new.astype(BF16)

    def ag_send(way, d):
        hop = 1 if d == -1 else 2
        far = max(d, 0) + hop
        i = (far - 1) * 2 + (way + 1) // 2
        part = gathered.at[ring(-way * max(d, 0)), xl]
        send(part, part, ag_s.at[i], ag_r.at[i], on_ring(way * hop))

    def cross(way, d):
        i = d * 2 + (way + 1) // 2 - 1
        t = ring(-way * d)
        for c, to in ((1, partner), (0, across)):
            part = gathered.at[t, xl, c]
            send(part, part, x_s.at[c, i], x_r.at[i], to)
        part = gathered.at[t, xl, 0]
        send(part, part, c_s.at[i], c_r.at[i], sibling)

    def ag_start():
        for d in (-1, 0):
            for way in (1, -1):
                ag_send(way, d)
        cross(1, 0)

    def ag_step(k):
        for d in (2 * k + 1, 2 * k + 2):
            for way in (1, -1):
                if d <= AG_FAR[way]:
                    i = (d - 1) * 2 + (way + 1) // 2
                    arrive(gathered.at[ring(-way * d), xl], ag_r.at[i])
                    if d + 2 <= AG_FAR[way]:
                        ag_send(way, d)
                    cross(way, d)

    def ag_crossed():
        for d in range(9):
            for way in (1, -1):
                if d <= AG_FAR[way] and (d, way) != (0, -1):
                    i, t = d * 2 + (way + 1) // 2 - 1, ring(-way * d)
                    arrive(gathered.at[t, 1 - xl, core], x_r.at[i])

    def ag_other_core():
        for d in range(9):
            for way in (1, -1):
                if d <= AG_FAR[way] and (d, way) != (0, -1):
                    i, t = d * 2 + (way + 1) // 2 - 1, ring(-way * d)
                    arrive(gathered.at[t, xl, 0], c_r.at[i])

    def key_send(name, part, to):
        i = KEYS.index(name)
        send(part, part, key_s.at[i], key_r.at[i], to)

    def key_arrive(name, part):
        arrive(part, key_r.at[KEYS.index(name)])

    def block(dy, dx):
        return keys_v.at[chip(dy, dx)]

    def keys_own():
        key_send("own", keys_v.at[chip(0, 0), core], sibling)

    def keys_start():
        key_arrive("own", keys_v.at[chip(0, 0), 1])
        key_send("up0", block(0, 0), in_group(1, 0, 0))
        key_send("down0", block(0, 0), in_group(3, 0, 0))
        key_send("x", block(0, 0), in_group(0, 1, 0))

    def keys_x():
        key_arrive("x", block(0, 1))
        key_send("up1", block(0, 1), in_group(1, 0, 0))
        key_send("down1", block(0, 1), in_group(3, 0, 0))
        key_send("s01", block(0, 1), sibling)

    def keys_y(dx):
        n = str(dx)
        key_arrive("up" + n, block(3, dx))
        key_send("upup" + n, keys_v.at[chip(3, dx), 0], in_group(1, 0, 0))
        key_send("s3" + n, block(3, dx), sibling)
        key_arrive("down" + n, block(1, dx))
        key_send("downdown" + n, keys_v.at[chip(1, dx), 1], in_group(3, 0, 0))
        key_send("s1" + n, block(1, dx), sibling)

    def keys_far(dx):
        n = str(dx)
        key_arrive("upup" + n, keys_v.at[chip(2, dx), 0])
        key_arrive("downdown" + n, keys_v.at[chip(2, dx), 1])
        key_send("s2" + n, block(2, dx), sibling)

    def keys_other_core(dx):
        for dy in (0, 1, 3, 2):
            if (dy, dx) != (0, 0):
                key_arrive("s%d%d" % (dy, dx), block(dy, dx))

    def statistics():
        @pl.loop(0, TOK // 16)
        def _(i):
            rows = pl.ds(pl.multiple_of(i * 16, 16), 16)
            total = jnp.zeros((16, 512), F32)
            for b in range(D // 512):
                v = hid_v[rows, b * 512 : (b + 1) * 512].astype(F32)
                total = total + v * v
            mean = jnp.sum(total, axis=-1, keepdims=True) * (1.0 / D)
            inv_v[rows, :] = jnp.broadcast_to(lax.rsqrt(mean + 1e-05), (16, 128))

    def normed(b, k):
        cols = pl.ds(pl.multiple_of(b * ROWS + k * 128, 128), 128)
        return (hid_v[:, cols].astype(F32) * inv_v[...] * gain_v[:, cols]).astype(BF16)

    def a2a_send(first, last):
        for i in range(first, last):
            dev = in_group(*PLACES[i])
            for k in range(ROWS // 128):
                send_v[i, :, k * 128 : (k + 1) * 128] = normed(dev[1], k)
            send(send_v.at[i], norm_v.at[chip(0, 0), core], a2a_s.at[i], a2a_r.at[i], dev)

    def own_block():
        for k in range(ROWS // 128):
            norm_v[chip(0, 0), core, :, k * 128 : (k + 1) * 128] = normed(fs, k)

    def multiply(dx):
        for i, (dy, px, dc) in enumerate(PLACES):
            if px == dx:
                arrive(norm_v.at[chip(-dy + 4, dx), (core + dc) % 2], a2a_r.at[i])
        base = ((xh + dx) % 2) * 4

        @pl.loop(0, 4)
        def _(i):
            rows = pl.ds(pl.multiple_of(i * (X // 4), X // 4), X // 4)
            left = jnp.concatenate([keys_v[base + q, c, rows, :] for q in range(4) for c in range(2)], axis=1)
            right = norm_v[pl.ds(base, 4)].reshape(8 * TOK, ROWS)
            part = jnp.dot(left, right, preferred_element_type=F32)
            acc[rows, :] = acc[rows, :] + part if dx else part

    stores = []

    def store(src, dst):
        cp = pltpu.make_async_copy(src, dst, store_sem.at[len(stores)])
        cp.start()
        stores.append(cp)

    def finish():
        scale = 1.0 / D**0.5
        for m in range(8):
            rows = pl.ds(m * 128, 128)
            old = wt[2 * m : 2 * m + 2].reshape(128, ROWS).astype(F32)
            new = gathered[2 * m : 2 * m + 2, :, core].reshape(128, ROWS).astype(F32)
            stepped = old - 1.0 * (acc[rows, :] * scale)
            out_v[:, m * 128 : (m + 1) * 128] = (0.5 * stepped + 0.5 * new).astype(BF16).T
            store(out_v.at[:, rows], merged.at[:, rows])

    def drain():
        for cp in stores:
            cp.wait()
        for cp in started:
            cp.wait_send()
        stores.clear()
        started.clear()

    @pl.when(core == 0)
    def _():
        send(wt.at[:, xl], other_wt, core_s.at[0], core_r.at[0], sibling)
        pair_send(across)
        keys_own()
        send(outer_v.at[0], outer_v.at[0], core_s.at[1], core_r.at[1], sibling)
        send(mom_v.at[0], mom_v.at[0], core_s.at[2], core_r.at[2], sibling)
        keys_start()
        statistics()
        a2a_send(0, 7)
        keys_x()
        a2a_send(7, 9)
        keys_y(0)
        a2a_send(9, 15)
        own_block()
        keys_y(1)
        keys_far(0)
        multiply(0)
        keys_far(1)
        multiply(1)
        arrive(on_v.at[0], core_r.at[3])
        arrive(mn_v.at[0], core_r.at[4])
        store(on_v.at[0], outer_new)
        store(mn_v.at[0], mom_new)
        ag_other_core()
        ag_crossed()
        finish()
        drain()

    @pl.when(core == 1)
    def _():
        pair_send(partner)
        keys_own()
        statistics()
        a2a_send(0, 4)
        arrive(other_wt, core_r.at[0])
        neighbours_are_in()
        rs_step(0)
        a2a_send(4, 10)
        rs_step(1)
        a2a_send(10, 15)
        own_block()
        rs_step(2)
        rs_step(3)
        update()
        ag_start()
        send(on_v.at[0], on_v.at[0], core_s.at[3], core_r.at[3], sibling)
        send(mn_v.at[0], mn_v.at[0], core_s.at[4], core_r.at[4], sibling)
        store(on_v.at[1], outer_new)
        store(mn_v.at[1], mom_new)
        for k in range(3):
            ag_step(k)
        key_arrive("own", keys_v.at[chip(0, 0), 0])
        keys_other_core(0)
        multiply(0)
        ag_step(3)
        keys_other_core(1)
        multiply(1)
        ag_crossed()
        finish()
        drain()


def copy_kernel(merged, outer_new, mom_new, merged_out, outer_out, mom_out, merged_v, outer_v, mom_v, in_sem, out_sem):
    routes = [(merged.at[r], merged_v.at[r], merged_out.at[r]) for r in (pl.ds(128 * i, 128) for i in range(4))]
    routes += [(outer_new, outer_v, outer_out), (mom_new, mom_v, mom_out)]
    arrive = [pltpu.make_async_copy(a, b, in_sem.at[i]) for i, (a, b, _) in enumerate(routes)]
    leave = [pltpu.make_async_copy(b, c, out_sem.at[i]) for i, (_, b, c) in enumerate(routes)]
    for cp in arrive:
        cp.start()
    for a, b in zip(arrive, leave):
        a.wait()
        b.start()
    for cp in leave:
        cp.wait()


def on_device(hidden, norm_gain, dkeys, local_weights, outer_params, momentum, sync_step):
    any_ = pl.BlockSpec(memory_space=pltpu.HBM)
    dma = pltpu.SemaphoreType.DMA
    merged, outer_new, mom_new = pl.pallas_call(
        kernel,
        out_shape=[
            jax.ShapeDtypeStruct((ROWS, X), BF16),
            jax.ShapeDtypeStruct((HALF, ROWS), F32),
            jax.ShapeDtypeStruct((HALF, ROWS), F32),
        ],
        in_specs=[pl.BlockSpec(memory_space=pltpu.SMEM)] + [any_] * 6,
        out_specs=[any_] * 3,
        scratch_shapes=[
            pltpu.VMEM((TOK, D), BF16),
            pltpu.VMEM((1, D), F32),
            pltpu.VMEM((TOK, X), BF16),
            pltpu.VMEM((ROWS, X), BF16),
            pltpu.VMEM((2, HALF, ROWS), F32),
            pltpu.VMEM((2, HALF, ROWS), F32),
            pltpu.VMEM((TOK, 128), F32),
            pltpu.VMEM((15, TOK, ROWS), BF16),
            pltpu.VMEM((8, 2, TOK, ROWS), BF16),
            pltpu.VMEM((8, 2, X, TOK), BF16),
            pltpu.VMEM((RING, 2, HALF, ROWS), BF16),
            pltpu.VMEM((RING, HALF, ROWS), BF16),
            pltpu.VMEM((2, RING, HALF, ROWS), BF16),
            pltpu.VMEM((4, 2, HALF, ROWS), BF16),
            pltpu.VMEM((15, 2, HALF, ROWS), BF16),
            pltpu.VMEM((RING, 2, 2, HALF, ROWS), BF16),
            pltpu.VMEM((X, ROWS), F32),
            pltpu.VMEM((ROWS, X), BF16),
            pltpu.VMEM((2, HALF, ROWS), F32),
            pltpu.VMEM((2, HALF, ROWS), F32),
            dma((6,)), dma((10,)), dma((15,)), dma((15,)), dma((17,)), dma((17,)), dma((16,)), dma((2, 16)),
            dma((5,)), dma((5,)), dma((15,)), dma((15,)), dma((16,)), dma((16,)),
            dma((2, 17)), dma((17,)), dma((17,)), dma((17,)), pltpu.SemaphoreType.REGULAR,
        ],
        compiler_params=pltpu.CompilerParams(
            collective_id=0, has_side_effects=True, vmem_limit_bytes=60 << 20
        ),
        name="outer_sync",
    )(
        sync_step, hidden[0], norm_gain.reshape(1, D), dkeys[0], local_weights[0],
        outer_params.T, momentum.T,
    )
    results = [merged, outer_new, mom_new]
    merged, outer_new, mom_new = pl.pallas_call(
        copy_kernel,
        out_shape=[jax.ShapeDtypeStruct(a.shape, a.dtype) for a in results],
        in_specs=[any_] * 3,
        out_specs=[any_] * 3,
        scratch_shapes=[pltpu.VMEM(a.shape, a.dtype) for a in results] + [dma((6,)), dma((6,))],
        compiler_params=pltpu.CompilerParams(vmem_limit_bytes=60 << 20),
        name="results",
    )(*results)
    return merged[None], outer_new.T, mom_new.T


def solution(mesh):
    placed = (
        P("replica", "fsdp", None),
        P(),
        P("replica", "fsdp", None),
        P("replica", "fsdp", None),
        P("fsdp", "replica"),
        P("fsdp", "replica"),
        P(),
    )
    return jax.shard_map(
        on_device,
        mesh=mesh,
        in_specs=placed,
        out_specs=(P("replica", "fsdp", None), P("fsdp", "replica"), P("fsdp", "replica")),
        check_vma=False,
    )
```

```python
import jax
import jax.numpy as jnp
from jax import lax
from jax.experimental import pallas as pl
from jax.experimental.pallas import tpu as pltpu
from jax.sharding import PartitionSpec as P

D = 8192
X = 1024
WARMUP = 8
WORKERS = 32
RING = 16
ROWS = 512
TOK = 128
COLS = X // RING
HALF = COLS // 2
MESH = pl.DeviceIdType.MESH
F32 = jnp.float32
BF16 = jnp.bfloat16

PLACES = [(dy, dx, dc) for dx in (0, 1) for dy in (2, 1, 3, 0) for dc in (0, 1) if (dy, dx, dc) != (0, 0, 0)]
CHAINS = [(-1, (8, 6, 4, 2)), (-1, (7, 5, 3, 1)), (1, (7, 5, 3, 1)), (1, (6, 4, 2))]
AG_FAR = {1: 8, -1: 7}
PAIR_ORDER = [way * c[k] for k in range(4) for way, c in CHAINS if k < len(c)] + [0]
KEYS = ["own", "x"] + [n + d for d in "01" for n in ("up", "down", "upup", "downdown", "s3", "s1", "s2")] + ["s01"]


def kernel(
    step, hid, gain, dk, w, outer, mom,
    merged, outer_new, mom_new,
    hid_v, gain_v, dk_v, w_v, outer_v, mom_v,
    inv_v, send_v, norm_v, keys_v, wt, other_wt, pair_v, first_v, chain_v, gathered, acc, out_v, on_v, mn_v,
    load_sem, store_sem, a2a_s, a2a_r, key_s, key_r, pair_s, pair_r, core_s, core_r,
    rs_s, rs_r, ag_s, ag_r, x_s, x_r, c_s, c_r, go_sem,
):
    rep, fs = lax.axis_index("replica"), lax.axis_index("fsdp")
    z, xl = rep // 2, rep % 2
    y, xh, core = fs // 4, (fs // 2) % 2, fs % 2

    def ring(dz):
        return (z + dz + RING) % RING

    def in_group(dy, dx, dc):
        return (rep, ((y + dy) % 4) * 4 + ((xh + dx) % 2) * 2 + (core + dc) % 2)

    def on_ring(dz):
        return (ring(dz) * 2 + xl, fs)

    def chip(dy, dx):
        return ((xh + dx) % 2) * 4 + (y + dy) % 4

    sibling = (rep, fs + 1 - 2 * core)
    partner = (z * 2 + 1 - xl, fs)
    across = (z * 2 + 1 - xl, fs + 1 - 2 * core)

    barrier = pltpu.get_barrier_semaphore()
    group = [(rep, (fs // 2 + i) % 8 * 2) for i in range(8)] + [(partner[0], fs - core)]
    along = [on_ring(d) for d in (1, -1, 2, -2)]

    def greet(dev):
        pl.semaphore_signal(barrier, inc=1, device_id=dev, device_id_type=MESH)

    for dev in group[1:]:
        greet(dev)

    @pl.when(core == 1)
    def _():
        greet(group[0])
        for dev in along:
            greet(dev)

    def group_is_in():
        @pl.when(core == 0)
        def _():
            pl.semaphore_wait(barrier, 17)
            pl.semaphore_signal(go_sem, inc=1, device_id=sibling, device_id_type=MESH)

        @pl.when(core == 1)
        def _():
            pl.semaphore_wait(go_sem, 1)

    def neighbours_are_in():
        pl.semaphore_wait(barrier, len(along))

    loads = [
        pltpu.make_async_copy(a, b, load_sem.at[i])
        for i, (a, b) in enumerate(
            [
                (w, w_v), (dk, dk_v), (hid, hid_v), (gain, gain_v),
                (outer, outer_v.at[core]), (mom, mom_v.at[core]),
            ]
        )
    ]
    for cp in loads:
        cp.start()

    loads[0].wait()

    @pl.loop(0, X // 128)
    def _(j):
        cols = pl.ds(pl.multiple_of(j * 128, 128), 128)
        wt[pl.ds(2 * j, 2)] = w_v[:, cols].T.reshape(2, 2, HALF, ROWS)

    loads[1].wait()
    for j in range(X // 128):
        keys_v[chip(0, 0), core, pl.ds(j * 128, 128), :] = dk_v[:, j * 128 : (j + 1) * 128].T

    for cp in loads[2:]:
        cp.wait()

    group_is_in()

    started = []

    def send(src, dst, ss, rs, dev):
        cp = pltpu.make_async_remote_copy(
            src_ref=src, dst_ref=dst, send_sem=ss, recv_sem=rs, device_id=dev, device_id_type=MESH
        )
        cp.start()
        started.append(cp)

    def arrive(dst, rs):
        pltpu.make_async_remote_copy(
            src_ref=dst, dst_ref=dst, send_sem=rs, recv_sem=rs, device_id=sibling, device_id_type=MESH
        ).wait_recv()

    def pair_send(to):
        for i, dz in enumerate(PAIR_ORDER):
            t = ring(dz)
            send(wt.at[t, 1 - xl], pair_v.at[core, t], pair_s.at[i], pair_r.at[core, i], to)

    def pair_sum(dz):
        t, i = ring(dz), PAIR_ORDER.index(dz)
        for c in (0, 1):
            arrive(pair_v.at[c, t], pair_r.at[c, i])
        return [
            other_wt[t].astype(F32) + pair_v[0, t].astype(F32),
            wt[t, xl].astype(F32) + pair_v[1, t].astype(F32),
        ]

    def rs_step(k):
        for n, (way, distances) in enumerate(CHAINS):
            if k >= len(distances):
                continue
            d = distances[k]
            i = n * 4 + k
            parts = pair_sum(way * d)
            if k == 0:
                buffer, at = first_v, n
            else:
                buffer, at = chain_v, i - 1
                arrive(chain_v.at[i - 1], rs_r.at[i - 1])
            for c in (0, 1):
                part = parts[c] if k == 0 else parts[c] + chain_v[i - 1, c].astype(F32)
                buffer[at, c] = part.astype(BF16)
            send(buffer.at[at], chain_v.at[i], rs_s.at[i], rs_r.at[i], on_ring(way * min(d, 2)))

    def update():
        totals = pair_sum(0)
        for n, (_, distances) in enumerate(CHAINS):
            i = n * 4 + len(distances) - 1
            arrive(chain_v.at[i], rs_r.at[i])
            totals = [totals[c] + chain_v[i, c].astype(F32) for c in (0, 1)]
        rate = 0.7 * jnp.minimum(1.0, (step[0].astype(F32) + 1.0) / WARMUP)
        arrive(outer_v.at[0], core_r.at[1])
        arrive(mom_v.at[0], core_r.at[2])
        for c in (0, 1):
            average = outer_v[c] - totals[c] / WORKERS
            momentum = 0.9 * mom_v[c] + average
            new = outer_v[c] - rate * (average + 0.9 * momentum)
            mn_v[c] = momentum
            on_v[c] = new
            gathered[z, xl, c] = new.astype(BF16)

    def ag_send(way, d):
        hop = 1 if d == -1 else 2
        far = max(d, 0) + hop
        i = (far - 1) * 2 + (way + 1) // 2
        part = gathered.at[ring(-way * max(d, 0)), xl]
        send(part, part, ag_s.at[i], ag_r.at[i], on_ring(way * hop))

    def cross(way, d):
        i = d * 2 + (way + 1) // 2 - 1
        t = ring(-way * d)
        for c, to in ((1, partner), (0, across)):
            part = gathered.at[t, xl, c]
            send(part, part, x_s.at[c, i], x_r.at[i], to)
        part = gathered.at[t, xl, 0]
        send(part, part, c_s.at[i], c_r.at[i], sibling)

    def ag_start():
        for d in (-1, 0):
            for way in (1, -1):
                ag_send(way, d)
        cross(1, 0)

    def ag_step(k):
        for d in (2 * k + 1, 2 * k + 2):
            for way in (1, -1):
                if d <= AG_FAR[way]:
                    i = (d - 1) * 2 + (way + 1) // 2
                    arrive(gathered.at[ring(-way * d), xl], ag_r.at[i])
                    if d + 2 <= AG_FAR[way]:
                        ag_send(way, d)
                    cross(way, d)

    def ag_crossed():
        for d in range(9):
            for way in (1, -1):
                if d <= AG_FAR[way] and (d, way) != (0, -1):
                    i, t = d * 2 + (way + 1) // 2 - 1, ring(-way * d)
                    arrive(gathered.at[t, 1 - xl, core], x_r.at[i])

    def ag_other_core():
        for d in range(9):
            for way in (1, -1):
                if d <= AG_FAR[way] and (d, way) != (0, -1):
                    i, t = d * 2 + (way + 1) // 2 - 1, ring(-way * d)
                    arrive(gathered.at[t, xl, 0], c_r.at[i])

    def key_send(name, part, to):
        i = KEYS.index(name)
        send(part, part, key_s.at[i], key_r.at[i], to)

    def key_arrive(name, part):
        arrive(part, key_r.at[KEYS.index(name)])

    def block(dy, dx):
        return keys_v.at[chip(dy, dx)]

    def keys_own():
        key_send("own", keys_v.at[chip(0, 0), core], sibling)

    def keys_start():
        key_arrive("own", keys_v.at[chip(0, 0), 1])
        key_send("up0", block(0, 0), in_group(1, 0, 0))
        key_send("down0", block(0, 0), in_group(3, 0, 0))
        key_send("x", block(0, 0), in_group(0, 1, 0))

    def keys_x():
        key_arrive("x", block(0, 1))
        key_send("up1", block(0, 1), in_group(1, 0, 0))
        key_send("down1", block(0, 1), in_group(3, 0, 0))
        key_send("s01", block(0, 1), sibling)

    def keys_y(dx):
        n = str(dx)
        key_arrive("up" + n, block(3, dx))
        key_send("upup" + n, keys_v.at[chip(3, dx), 0], in_group(1, 0, 0))
        key_send("s3" + n, block(3, dx), sibling)
        key_arrive("down" + n, block(1, dx))
        key_send("downdown" + n, keys_v.at[chip(1, dx), 1], in_group(3, 0, 0))
        key_send("s1" + n, block(1, dx), sibling)

    def keys_far(dx):
        n = str(dx)
        key_arrive("upup" + n, keys_v.at[chip(2, dx), 0])
        key_arrive("downdown" + n, keys_v.at[chip(2, dx), 1])
        key_send("s2" + n, block(2, dx), sibling)

    def keys_other_core(dx):
        for dy in (0, 1, 3, 2):
            if (dy, dx) != (0, 0):
                key_arrive("s%d%d" % (dy, dx), block(dy, dx))

    def statistics():
        @pl.loop(0, TOK // 16)
        def _(i):
            rows = pl.ds(pl.multiple_of(i * 16, 16), 16)
            total = jnp.zeros((16, 512), F32)
            for b in range(D // 512):
                v = hid_v[rows, b * 512 : (b + 1) * 512].astype(F32)
                total = total + v * v
            mean = jnp.sum(total, axis=-1, keepdims=True) * (1.0 / D)
            inv_v[rows, :] = jnp.broadcast_to(lax.rsqrt(mean + 1e-05), (16, 128))

    def normed(b, k):
        cols = pl.ds(pl.multiple_of(b * ROWS + k * 128, 128), 128)
        return (hid_v[:, cols].astype(F32) * inv_v[...] * gain_v[:, cols]).astype(BF16)

    def a2a_send(first, last):
        for i in range(first, last):
            dev = in_group(*PLACES[i])
            for k in range(ROWS // 128):
                send_v[i, :, k * 128 : (k + 1) * 128] = normed(dev[1], k)
            send(send_v.at[i], norm_v.at[chip(0, 0), core], a2a_s.at[i], a2a_r.at[i], dev)

    def own_block():
        for k in range(ROWS // 128):
            norm_v[chip(0, 0), core, :, k * 128 : (k + 1) * 128] = normed(fs, k)

    def multiply(dx):
        for i, (dy, px, dc) in enumerate(PLACES):
            if px == dx:
                arrive(norm_v.at[chip(-dy + 4, dx), (core + dc) % 2], a2a_r.at[i])
        base = ((xh + dx) % 2) * 4

        @pl.loop(0, 4)
        def _(i):
            rows = pl.ds(pl.multiple_of(i * (X // 4), X // 4), X // 4)
            left = jnp.concatenate([keys_v[base + q, c, rows, :] for q in range(4) for c in range(2)], axis=1)
            right = norm_v[pl.ds(base, 4)].reshape(8 * TOK, ROWS)
            part = jnp.dot(left, right, preferred_element_type=F32)
            acc[rows, :] = acc[rows, :] + part if dx else part

    stores = []

    def store(src, dst):
        cp = pltpu.make_async_copy(src, dst, store_sem.at[len(stores)])
        cp.start()
        stores.append(cp)

    def finish():
        scale = 1.0 / D**0.5
        for m in range(8):
            rows = pl.ds(m * 128, 128)
            old = wt[2 * m : 2 * m + 2].reshape(128, ROWS).astype(F32)
            new = gathered[2 * m : 2 * m + 2, :, core].reshape(128, ROWS).astype(F32)
            stepped = old - 1.0 * (acc[rows, :] * scale)
            out_v[:, m * 128 : (m + 1) * 128] = (0.5 * stepped + 0.5 * new).astype(BF16).T
            store(out_v.at[:, rows], merged.at[:, rows])

    def drain():
        for cp in stores:
            cp.wait()
        for cp in started:
            cp.wait_send()
        stores.clear()
        started.clear()

    @pl.when(core == 0)
    def _():
        send(wt.at[:, xl], other_wt, core_s.at[0], core_r.at[0], sibling)
        pair_send(across)
        keys_own()
        send(outer_v.at[0], outer_v.at[0], core_s.at[1], core_r.at[1], sibling)
        send(mom_v.at[0], mom_v.at[0], core_s.at[2], core_r.at[2], sibling)
        keys_start()
        statistics()
        a2a_send(0, 7)
        keys_x()
        a2a_send(7, 9)
        keys_y(0)
        a2a_send(9, 15)
        own_block()
        keys_y(1)
        keys_far(0)
        multiply(0)
        keys_far(1)
        multiply(1)
        arrive(on_v.at[0], core_r.at[3])
        arrive(mn_v.at[0], core_r.at[4])
        store(on_v.at[0], outer_new)
        store(mn_v.at[0], mom_new)
        ag_other_core()
        ag_crossed()
        finish()
        drain()

    @pl.when(core == 1)
    def _():
        pair_send(partner)
        keys_own()
        statistics()
        arrive(other_wt, core_r.at[0])
        a2a_send(0, 2)
        neighbours_are_in()
        rs_step(0)
        a2a_send(2, 7)
        rs_step(1)
        a2a_send(7, 15)
        own_block()
        rs_step(2)
        rs_step(3)
        update()
        ag_start()
        send(on_v.at[0], on_v.at[0], core_s.at[3], core_r.at[3], sibling)
        send(mn_v.at[0], mn_v.at[0], core_s.at[4], core_r.at[4], sibling)
        store(on_v.at[1], outer_new)
        store(mn_v.at[1], mom_new)
        for k in range(3):
            ag_step(k)
        key_arrive("own", keys_v.at[chip(0, 0), 0])
        keys_other_core(0)
        multiply(0)
        ag_step(3)
        keys_other_core(1)
        multiply(1)
        ag_crossed()
        finish()
        drain()


def copy_kernel(merged, outer_new, mom_new, merged_out, outer_out, mom_out, merged_v, outer_v, mom_v, in_sem, out_sem):
    routes = [(merged.at[r], merged_v.at[r], merged_out.at[r]) for r in (pl.ds(128 * i, 128) for i in range(4))]
    routes += [(outer_new, outer_v, outer_out), (mom_new, mom_v, mom_out)]
    arrive = [pltpu.make_async_copy(a, b, in_sem.at[i]) for i, (a, b, _) in enumerate(routes)]
    leave = [pltpu.make_async_copy(b, c, out_sem.at[i]) for i, (_, b, c) in enumerate(routes)]
    for cp in arrive:
        cp.start()
    for a, b in zip(arrive, leave):
        a.wait()
        b.start()
    for cp in leave:
        cp.wait()


def on_device(hidden, norm_gain, dkeys, local_weights, outer_params, momentum, sync_step):
    any_ = pl.BlockSpec(memory_space=pltpu.HBM)
    dma = pltpu.SemaphoreType.DMA
    merged, outer_new, mom_new = pl.pallas_call(
        kernel,
        out_shape=[
            jax.ShapeDtypeStruct((ROWS, X), BF16),
            jax.ShapeDtypeStruct((HALF, ROWS), F32),
            jax.ShapeDtypeStruct((HALF, ROWS), F32),
        ],
        in_specs=[pl.BlockSpec(memory_space=pltpu.SMEM)] + [any_] * 6,
        out_specs=[any_] * 3,
        scratch_shapes=[
            pltpu.VMEM((TOK, D), BF16),
            pltpu.VMEM((1, D), F32),
            pltpu.VMEM((TOK, X), BF16),
            pltpu.VMEM((ROWS, X), BF16),
            pltpu.VMEM((2, HALF, ROWS), F32),
            pltpu.VMEM((2, HALF, ROWS), F32),
            pltpu.VMEM((TOK, 128), F32),
            pltpu.VMEM((15, TOK, ROWS), BF16),
            pltpu.VMEM((8, 2, TOK, ROWS), BF16),
            pltpu.VMEM((8, 2, X, TOK), BF16),
            pltpu.VMEM((RING, 2, HALF, ROWS), BF16),
            pltpu.VMEM((RING, HALF, ROWS), BF16),
            pltpu.VMEM((2, RING, HALF, ROWS), BF16),
            pltpu.VMEM((4, 2, HALF, ROWS), BF16),
            pltpu.VMEM((15, 2, HALF, ROWS), BF16),
            pltpu.VMEM((RING, 2, 2, HALF, ROWS), BF16),
            pltpu.VMEM((X, ROWS), F32),
            pltpu.VMEM((ROWS, X), BF16),
            pltpu.VMEM((2, HALF, ROWS), F32),
            pltpu.VMEM((2, HALF, ROWS), F32),
            dma((6,)), dma((10,)), dma((15,)), dma((15,)), dma((17,)), dma((17,)), dma((16,)), dma((2, 16)),
            dma((5,)), dma((5,)), dma((15,)), dma((15,)), dma((16,)), dma((16,)),
            dma((2, 17)), dma((17,)), dma((17,)), dma((17,)), pltpu.SemaphoreType.REGULAR,
        ],
        compiler_params=pltpu.CompilerParams(
            collective_id=0, has_side_effects=True, vmem_limit_bytes=60 << 20
        ),
        name="outer_sync",
    )(
        sync_step, hidden[0], norm_gain.reshape(1, D), dkeys[0], local_weights[0],
        outer_params.T, momentum.T,
    )
    results = [merged, outer_new, mom_new]
    merged, outer_new, mom_new = pl.pallas_call(
        copy_kernel,
        out_shape=[jax.ShapeDtypeStruct(a.shape, a.dtype) for a in results],
        in_specs=[any_] * 3,
        out_specs=[any_] * 3,
        scratch_shapes=[pltpu.VMEM(a.shape, a.dtype) for a in results] + [dma((6,)), dma((6,))],
        compiler_params=pltpu.CompilerParams(vmem_limit_bytes=60 << 20),
        name="results",
    )(*results)
    return merged[None], outer_new.T, mom_new.T


def solution(mesh):
    placed = (
        P("replica", "fsdp", None),
        P(),
        P("replica", "fsdp", None),
        P("replica", "fsdp", None),
        P("fsdp", "replica"),
        P("fsdp", "replica"),
        P(),
    )
    return jax.shard_map(
        on_device,
        mesh=mesh,
        in_specs=placed,
        out_specs=(P("replica", "fsdp", None), P("fsdp", "replica"), P("fsdp", "replica")),
        check_vma=False,
    )
```
